32 devices in a mesh: row: 8 (over y, x, core), col: 4 (over z).
Axes of the slice: x: 2, y: 2, z: 4, core: 2. Of those that a mesh axis runs over, the one named last changes fastest.
Arguments:
- node_features: bfloat16 [8192, 256], P(('row', 'col')), may hold values from -6 to 6
- tile_values: bfloat16 [8, 4, 128, 128, 128], P('row', 'col'), may hold values from -0.09375 to 0.09375
- tile_coords: int32 [8, 4, 128, 2], P('row', 'col'), may hold values from 0 to 15, as said below
- tile_counts: int32 [8, 4], P('row', 'col'), may hold values from 32 to 128, as said below
- first_weight: bfloat16 [256, 256], replicated, may hold values from -0.375 to 0.375
- second_weight: bfloat16 [256, 128], replicated, may hold values from -0.375 to 0.375
- out_grad: bfloat16 [8192, 128], P(('row', 'col')), may hold values from -6 to 6
Outputs:
- output: bfloat16 [8192, 128], P(('row', 'col'))
- first_grad: float32 [256, 256], replicated
- second_grad: float32 [256, 128], replicated
The draws below stay inside these ranges and needn't reach their ends.
Inputs may be any that keep to these rules, and one draw needn't show every extreme that they name: `tile_counts`: each grid cell uses at least 32 slots; at least one grid cell uses all 128 in every draw. `tile_coords`: the first entry is a tile row below 16, the second a tile column below 8; within one grid cell no two slots share a position.
All inputs are finite; a program needn't handle non-finite values.
Results may differ from the reference program's by a relative error of at most 0.005.
Values may be sent and summed in bfloat16 or wider, within the bound.
No kernel may reach another device: no remote copies, remote signals or barrier semaphores. Data moves between devices by JAX's collectives and lax.ppermute only.
A program may use at most 64 MiB of HBM per device.

```python
import math
import jax
import jax.numpy as jnp
from jax import lax

TILE = 128
FEAT = 256
HIDDEN_SIZE = 256
CLASSES = 128
NODE_DEV = 256
MAXT = 128
GRID_ROWS = 8
GRID_COLS = 4
ROW_TILES = 16
COL_TILES = 8
NODES = 8192


def draw_tile_counts(key, part):
    grid_rows = ROW_TILES * TILE // NODE_DEV
    grid_cols = COL_TILES * TILE // NODE_DEV
    count_key, place_key = jax.random.split(key)
    raw_draw = jax.random.randint(count_key, (grid_rows * grid_cols,), 0, MAXT + 1)
    counted = MAXT // 4 + 3 * raw_draw * raw_draw // (4 * MAXT)
    fullest = jax.random.randint(place_key, (), 0, grid_rows * grid_cols)
    counted = counted.at[fullest].set(MAXT)
    return counted.reshape(grid_rows, grid_cols).astype(jnp.int32)


def draw_tile_coords(key, part):
    grid_rows = ROW_TILES * TILE // NODE_DEV
    grid_cols = COL_TILES * TILE // NODE_DEV
    cell_keys = jax.random.split(jax.random.fold_in(key, 7), grid_rows * grid_cols)

    def pick_cell(cell_key):
        return jax.random.permutation(cell_key, ROW_TILES * COL_TILES)[:MAXT]
    places = jax.vmap(pick_cell)(cell_keys).astype(jnp.int32)
    coords = jnp.stack([places // COL_TILES, places % COL_TILES], axis=-1)
    return coords.reshape(grid_rows, grid_cols, MAXT, 2).astype(jnp.int32)


def level_of(own_key, dims, shards, least, largest):
    level, own = 1.0, jax.random.fold_in(own_key, 6)
    for position, shards_of in shards:
        draws = jnp.exp(jax.random.uniform(jax.random.fold_in(own, position), (shards_of,), jnp.float32, least / len(shards), largest / len(shards)))
        level = level * jnp.repeat(draws, dims[position] // shards_of).reshape([-1 if axis == position else 1 for axis in range(len(dims))])
    return level


def scatter_about(rng, extent, deviation, limit, shards=(), held_as=jnp.bfloat16):
    array = deviation * jax.random.normal(rng, extent, jnp.float32)
    if shards:
        array = array * level_of(rng, extent, shards, -0.22, 0.18)
    return jnp.clip(array, -limit, limit).astype(held_as)


def setup_inputs(seed: int = 0) -> dict:
    splits = jax.random.split(jax.random.key(seed), 8)
    return {
        "node_features": scatter_about(splits[0], (NODES, FEAT), 1.0, 6.0, ((0, 32),)),
        "tile_values": scatter_about(splits[1], (GRID_ROWS, GRID_COLS, MAXT, TILE, TILE), (TILE * TILE * MAXT // (2 * NODE_DEV)) ** -0.5, 0.09375, ((0, 8), (1, 4))),
        "tile_coords": draw_tile_coords(jax.random.fold_in(splits[7], 71), 0),
        "tile_counts": draw_tile_counts(jax.random.fold_in(splits[7], 71), 0),
        "first_weight": scatter_about(splits[4], (FEAT, HIDDEN_SIZE), FEAT ** -0.5, 0.375),
        "second_weight": scatter_about(splits[5], (HIDDEN_SIZE, CLASSES), HIDDEN_SIZE ** -0.5, 0.375),
        "out_grad": scatter_about(splits[6], (NODES, CLASSES), 1.0, 6.0, ((0, 32),)),
    }


HIGHEST = lax.Precision.HIGHEST

def forward_sum(tile_values, tile_coords, tile_counts, features):
    width = features.shape[-1]
    grid_feat = features.astype(jnp.float32).reshape(GRID_ROWS, COL_TILES, TILE, width)
    slot_ids = jnp.arange(MAXT, dtype=jnp.int32)
    row_ids = jnp.arange(ROW_TILES, dtype=jnp.int32)

    def one_row(total, pieces):
        tile_row, coord_row, count_row, source = pieces
        picked = source[coord_row[:, :, 1]]
        products = jnp.einsum('jtab,jtbw->jtaw', tile_row.astype(jnp.float32), picked, precision=HIGHEST)
        alive = slot_ids[None, :] < count_row[:, None]
        select = ((coord_row[:, :, 0][:, :, None] == row_ids[None, None, :]) & alive[:, :, None]).astype(jnp.float32)
        return (total + jnp.einsum('jtr,jtaw->jraw', select, products, precision=HIGHEST), None)
    start_sum = jnp.zeros((GRID_COLS, ROW_TILES, TILE, width), jnp.float32)
    total, unused = lax.scan(one_row, start_sum, (tile_values, tile_coords, tile_counts, grid_feat))
    total = total.reshape(GRID_COLS, GRID_ROWS, NODE_DEV, width).transpose(1, 0, 2, 3)
    return total.reshape(NODES, width)

def backward_sum(tile_values, tile_coords, tile_counts, features):
    width = features.shape[-1]
    grid_feat = features.astype(jnp.float32).reshape(GRID_ROWS, GRID_COLS, NODE_DEV, width)
    grid_feat = grid_feat.transpose(1, 0, 2, 3).reshape(GRID_COLS, ROW_TILES, TILE, width)
    slot_ids = jnp.arange(MAXT, dtype=jnp.int32)
    col_ids = jnp.arange(COL_TILES, dtype=jnp.int32)
    cell_ids = jnp.arange(GRID_COLS, dtype=jnp.int32)

    def one_row(carry, pieces):
        tile_row, coord_row, count_row = pieces
        picked = grid_feat[cell_ids[:, None], coord_row[:, :, 0]]
        products = jnp.einsum('jtab,jtaw->jtbw', tile_row.astype(jnp.float32), picked, precision=HIGHEST)
        alive = slot_ids[None, :] < count_row[:, None]
        select = ((coord_row[:, :, 1][:, :, None] == col_ids[None, None, :]) & alive[:, :, None]).astype(jnp.float32)
        return (carry, jnp.einsum('jtr,jtbw->rbw', select, products, precision=HIGHEST))
    unused, rows_out = lax.scan(one_row, jnp.zeros((), jnp.float32), (tile_values, tile_coords, tile_counts))
    return rows_out.reshape(NODES, width)

def reference(node_features, tile_values, tile_coords, tile_counts, first_weight, second_weight, out_grad):
    first_mean = forward_sum(tile_values, tile_coords, tile_counts, node_features)
    first_pre = jnp.dot(first_mean, first_weight.astype(jnp.float32), precision=HIGHEST)
    hidden_act = jax.nn.silu(first_pre).astype(jnp.bfloat16)
    second_mean = forward_sum(tile_values, tile_coords, tile_counts, hidden_act)
    output = jnp.dot(second_mean, second_weight.astype(jnp.float32), precision=HIGHEST).astype(jnp.bfloat16)
    back_sum = backward_sum(tile_values, tile_coords, tile_counts, out_grad)
    hidden_grad = jnp.dot(back_sum, second_weight.astype(jnp.float32).T, precision=HIGHEST)
    sigma = jax.nn.sigmoid(first_pre)
    pre_grad = hidden_grad * (sigma * (1.0 + first_pre * (1.0 - sigma)))
    scale = 1.0 / math.sqrt(NODES)
    first_grad = jnp.dot(first_mean.T, pre_grad, precision=HIGHEST) * scale
    second_grad = jnp.dot(hidden_act.astype(jnp.float32).T, back_sum, precision=HIGHEST) * scale
    return (output, first_grad, second_grad)
```

```python
import functools
import math

import jax
import jax.numpy as jnp
from jax import lax
from jax.experimental import pallas as pl
from jax.experimental.pallas import tpu as pltpu
from jax.sharding import PartitionSpec as P

BF16 = jnp.bfloat16
F32 = jnp.float32


def assemble_kernel(places_ref, count_ref, tiles_ref, dense_ref, sems):
    slots, edge = tiles_ref.shape[0], tiles_ref.shape[1]
    live = count_ref[0]
    strip = min(dense_ref.shape[1], 256)

    def clear(step, carry):
        rows = pl.ds(pl.multiple_of(step * strip, strip), strip)
        for half in range(2):
            dense_ref[half, rows, :] = jnp.zeros((strip, dense_ref.shape[2]), BF16)
        return carry

    lax.fori_loop(0, dense_ref.shape[1] // strip, clear, 0)

    def tile_copy(slot):
        rows = pl.ds(pl.multiple_of(places_ref[1, slot] * edge, edge), edge)
        cols = pl.ds(pl.multiple_of(places_ref[2, slot] * edge, edge), edge)
        return pltpu.make_async_copy(
            tiles_ref.at[slot], dense_ref.at[places_ref[0, slot], rows, cols], sems.at[slot]
        )

    def begin(slot, carry):
        @pl.when(slot < live)
        def _():
            tile_copy(slot).start()

        return carry

    def finish(slot, carry):
        @pl.when(slot < live)
        def _():
            tile_copy(slot).wait()

        return carry

    lax.fori_loop(0, slots, begin, 0)
    lax.fori_loop(0, slots, finish, 0)


def assemble(tiles, places, count, rows, cols):
    slots = tiles.shape[0]
    return pl.pallas_call(
        assemble_kernel,
        out_shape=jax.ShapeDtypeStruct((2, rows // 2, cols), BF16),
        in_specs=[
            pl.BlockSpec(memory_space=pltpu.SMEM),
            pl.BlockSpec(memory_space=pltpu.SMEM),
            pl.BlockSpec(memory_space=pl.ANY),
        ],
        out_specs=pl.BlockSpec(memory_space=pltpu.VMEM),
        scratch_shapes=[pltpu.SemaphoreType.DMA((slots,))],
        compiler_params=pltpu.CompilerParams(vmem_limit_bytes=rows * cols * 2 + (8 << 20)),
        cost_estimate=pl.CostEstimate(
            flops=0, bytes_accessed=2 * rows * cols * 2, transcendentals=0
        ),
    )(places, count, tiles)


def tree_sum(parts):
    parts = [part.astype(F32) for part in parts]
    while len(parts) > 1:
        parts = [parts[i] + parts[i + 1] for i in range(0, len(parts), 2)]
    return parts[0]


def swap(value, axis, offset):
    size = lax.axis_size(axis)
    return lax.ppermute(value, axis, [(i, i ^ offset) for i in range(size)])


def matmul(left, right, left_dim=1, right_dim=0):
    return lax.dot_general(
        left, right, (((left_dim,), (right_dim,)), ((), ())), preferred_element_type=F32
    )


def on_device(
    node_features, tile_values, tile_coords, tile_counts, first_weight, second_weight, out_grad
):
    node_rows = node_features.shape[0]
    edge = tile_values.shape[-1]
    slots = tile_values.shape[2]
    grid_rows = lax.axis_size("row")
    grid_cols = lax.axis_size("col")
    chips = grid_rows // 2
    per_node = node_rows // edge
    me_row = lax.axis_index("row")
    me_col = lax.axis_index("col")
    me_core = me_row % 2

    def gather_col(value):
        return jnp.concatenate(
            [value] + [swap(value, "col", k) for k in range(1, grid_cols)], axis=0
        )

    def gather_plane(value):
        return jnp.concatenate(
            [value] + [swap(value, "row", 2 * i) for i in range(1, chips)], axis=0
        )

    coords = tile_coords.reshape(slots, 2)
    tile_row, tile_col = coords[:, 0], coords[:, 1]
    offset = (tile_row // per_node) ^ me_row
    places = jnp.stack(
        [
            offset % 2,
            (offset // 2) * per_node + tile_row % per_node,
            ((tile_col // per_node) ^ me_col) * per_node + tile_col % per_node,
        ]
    )
    gathered_x = gather_col(node_features)
    grad_own = gather_plane(out_grad)
    grad_other = swap(grad_own, "row", 1)
    dense = assemble(
        tile_values.reshape(slots, edge, edge),
        places,
        tile_counts.reshape(1),
        grid_rows * node_rows,
        grid_cols * node_rows,
    )
    dense_own, dense_other = dense[0], dense[1]

    def reduce_plane(source):
        other = matmul(dense_other, source).astype(BF16)
        arrived = swap(other, "row", 1)
        chip_sum = matmul(dense_own, source) + arrived.astype(F32)
        blocks = chip_sum.reshape(chips, node_rows, -1)
        sent = [swap(blocks[i].astype(BF16), "row", 2 * i) for i in range(1, chips)]
        return tree_sum([blocks[0]] + sent)

    back_part = matmul(dense_own, grad_own, 0) + matmul(dense_other, grad_other, 0)
    back_blocks = back_part.reshape(grid_cols, node_rows, -1)
    back_sum = tree_sum(
        [back_blocks[0]]
        + [swap(back_blocks[k].astype(BF16), "col", k) for k in range(1, grid_cols)]
    )
    hidden_grad = matmul(back_sum.astype(BF16), second_weight, 1, 1)

    first_mean = reduce_plane(gathered_x)
    first_pre = matmul(first_mean.astype(BF16), first_weight)
    sigma = jax.nn.sigmoid(first_pre)
    hidden_act = (first_pre * sigma).astype(BF16)
    projected = matmul(hidden_act, second_weight).astype(BF16)
    output = reduce_plane(gather_col(projected)).astype(BF16)

    pre_grad = hidden_grad * (sigma * (1.0 + first_pre * (1.0 - sigma)))
    scale = 1.0 / math.sqrt(node_rows * grid_rows * grid_cols)
    first_local = matmul(first_mean.astype(BF16), pre_grad.astype(BF16), 0)
    second_local = matmul(hidden_act, back_sum.astype(BF16), 0)
    grads = jnp.concatenate([first_local, second_local], axis=1) * scale
    half = grads.shape[0] // 2
    low, high = grads[:half], grads[half:]
    mine = jnp.where(me_core == 0, low, high)
    theirs = jnp.where(me_core == 0, high, low)
    mine = (mine + swap(theirs.astype(BF16), "row", 1).astype(F32)).astype(BF16)
    mine = tree_sum([mine] + [swap(mine, "row", 2 * i) for i in range(1, chips)]).astype(BF16)
    mine = tree_sum([mine] + [swap(mine, "col", k) for k in range(1, grid_cols)])
    theirs = swap(mine, "row", 1)
    low = jnp.where(me_core == 0, mine, theirs)
    high = jnp.where(me_core == 0, theirs, mine)
    grads = jnp.concatenate([low, high], axis=0)
    width = first_weight.shape[1]
    return (output, grads[:, :width], grads[:, width:])


def solution(mesh):
    return jax.shard_map(
        on_device,
        mesh=mesh,
        in_specs=(
            P(("row", "col"), None),
            P("row", "col", None, None, None),
            P("row", "col", None, None),
            P("row", "col"),
            P(),
            P(),
            P(("row", "col"), None),
        ),
        out_specs=(P(("row", "col"), None), P(), P()),
        check_vma=False,
    )
```

```python
import math

import jax
import jax.numpy as jnp
from jax import lax
from jax.experimental import pallas as pl
from jax.experimental.pallas import tpu as pltpu
from jax.sharding import PartitionSpec as P

BF16 = jnp.bfloat16
F32 = jnp.float32


def dot_parts(left, right, left_dim=1, right_dim=0):
    def parts(value):
        if value.dtype == BF16:
            return [value]
        high = lax.reduce_precision(value, 8, 7)
        return [high.astype(BF16), (value - high).astype(BF16)]

    lefts, rights = parts(left), parts(right)
    total = None
    for i, one in enumerate(lefts):
        for j, other in enumerate(rights):
            if i + j < 2:
                term = lax.dot_general(
                    one, other, (((left_dim,), (right_dim,)), ((), ())), preferred_element_type=F32
                )
                total = term if total is None else total + term
    return total


def tree_sum(parts):
    parts = [part.astype(F32) for part in parts]
    while len(parts) > 1:
        parts = [parts[i] + parts[i + 1] for i in range(0, len(parts), 2)]
    return parts[0]


def assemble_kernel(per_node, coords_ref, count_ref, tiles_ref, dense_ref, sem):
    slots, edge = tiles_ref.shape[0], tiles_ref.shape[1]
    halves, rows, cols = dense_ref.shape
    me_row, me_col = lax.axis_index("row"), lax.axis_index("col")
    live = count_ref[0]
    strip = math.gcd(rows, 256)
    shift = per_node.bit_length() - 1

    @pl.when(live * edge * edge < halves * rows * cols)
    def _():
        def clear(step, carry):
            place = pl.ds(pl.multiple_of(step * strip, strip), strip)
            for half in range(halves):
                dense_ref[half, place, :] = jnp.zeros((strip, cols), BF16)
            return carry

        lax.fori_loop(0, rows // strip, clear, 0)

    def begin(slot):
        row, col = coords_ref[0, slot], coords_ref[1, slot]
        offset = (row >> shift) ^ me_row
        row_place = ((offset >> 1) << shift) + (row & (per_node - 1))
        col_place = (((col >> shift) ^ me_col) << shift) + (col & (per_node - 1))
        pltpu.make_async_copy(
            tiles_ref.at[slot],
            dense_ref.at[
                offset & 1,
                pl.ds(pl.multiple_of(row_place * edge, edge), edge),
                pl.ds(pl.multiple_of(col_place * edge, edge), edge),
            ],
            sem,
        ).start()

    def begin_group(step, carry):
        for i in range(8):
            begin(step * 8 + i)
        return carry

    def begin_one(slot, carry):
        begin(slot)
        return carry

    groups = live >> 3
    lax.fori_loop(0, groups, begin_group, 0)
    lax.fori_loop(groups << 3, live, begin_one, 0)
    size = 1
    while size <= slots:

        @pl.when((live & size) != 0)
        def _(size=size):
            some = tiles_ref.at[pl.ds(0, size)]
            pltpu.make_async_copy(some, some, sem).wait()

        size *= 2


def assemble(tiles, coords, count, rows, cols, per_node):
    def kernel(*refs):
        assemble_kernel(per_node, *refs)

    return pl.pallas_call(
        kernel,
        out_shape=jax.ShapeDtypeStruct((2, rows // 2, cols), BF16),
        in_specs=[
            pl.BlockSpec(memory_space=pltpu.SMEM),
            pl.BlockSpec(memory_space=pltpu.SMEM),
            pl.BlockSpec(memory_space=pltpu.HBM),
        ],
        out_specs=pl.BlockSpec(memory_space=pltpu.VMEM),
        scratch_shapes=[pltpu.SemaphoreType.DMA],
        compiler_params=pltpu.CompilerParams(vmem_limit_bytes=rows * cols * 2 + (2 << 20)),
        cost_estimate=pl.CostEstimate(
            flops=0, bytes_accessed=2 * rows * cols * 2, transcendentals=0
        ),
        name="assemble",
    )(coords, count, tiles)


def local_grads_kernel(scale, grid_cols, *refs):
    mean_ref, pre_ref, back_ref = refs[:3]
    arrived_refs = refs[3 : 2 + grid_cols]
    weight_ref, mine_ref, theirs_ref = refs[2 + grid_cols :]
    back_sum = tree_sum([back_ref[: mean_ref.shape[0], :]] + [ref[...] for ref in arrived_refs])
    hidden_grad = dot_parts(back_sum, weight_ref[...], 1, 1)
    first_pre = pre_ref[...]
    sigma = jax.nn.sigmoid(first_pre)
    hidden_act = (first_pre * sigma).astype(BF16)
    pre_grad = hidden_grad * (sigma * (1.0 + first_pre * (1.0 - sigma)))
    first = dot_parts(mean_ref[...], pre_grad, 0, 0) * scale
    second = dot_parts(hidden_act, back_sum, 0, 0) * scale
    half, width = mine_ref.shape[0], first.shape[1]
    low_core = lax.axis_index("row") % 2 == 0
    for value, place in ((first, slice(0, width)), (second, slice(width, None))):
        low, high = value[:half], value[half:]
        mine_ref[:, place] = jnp.where(low_core, low, high)
        theirs_ref[:, place] = jnp.where(low_core, high, low).astype(BF16)


def local_grads(mean, pre, back, arrived, weight, scale):
    grid_cols = len(arrived) + 1
    half = mean.shape[1] // 2
    width = pre.shape[1] + weight.shape[1]

    def kernel(*refs):
        local_grads_kernel(scale, grid_cols, *refs)

    vmem = pl.BlockSpec(memory_space=pltpu.VMEM)
    return pl.pallas_call(
        kernel,
        out_shape=(
            jax.ShapeDtypeStruct((half, width), F32),
            jax.ShapeDtypeStruct((half, width), BF16),
        ),
        in_specs=[vmem] * (4 + len(arrived)),
        out_specs=(vmem, vmem),
        compiler_params=pltpu.CompilerParams(vmem_limit_bytes=6 << 20),
        cost_estimate=pl.CostEstimate(
            flops=2 * 256 * 256 * 384 * 3, bytes_accessed=1 << 20, transcendentals=1 << 16
        ),
        name="local_grads",
    )(mean, pre, back, *arrived, weight)


def join_kernel(mine_ref, theirs_ref, first_ref, second_ref):
    half, width = mine_ref.shape[0], first_ref.shape[1]
    low_core = lax.axis_index("row") % 2 == 0
    for ref, place in ((first_ref, slice(0, width)), (second_ref, slice(width, None))):
        mine, theirs = mine_ref[:, place], theirs_ref[:, place]
        ref[:half, :] = jnp.where(low_core, mine, theirs)
        ref[half:, :] = jnp.where(low_core, theirs, mine)


def join(mine, theirs, width):
    vmem = pl.BlockSpec(memory_space=pltpu.VMEM)
    rows = 2 * mine.shape[0]
    return pl.pallas_call(
        join_kernel,
        out_shape=(
            jax.ShapeDtypeStruct((rows, width), F32),
            jax.ShapeDtypeStruct((rows, mine.shape[1] - width), F32),
        ),
        in_specs=[vmem, vmem],
        out_specs=(vmem, vmem),
        compiler_params=pltpu.CompilerParams(vmem_limit_bytes=2 << 20),
        name="join_grads",
    )(mine, theirs)


def swap(value, axis, offset):
    size = lax.axis_size(axis)
    return lax.ppermute(value, axis, [(i, i ^ offset) for i in range(size)])


def on_device(
    node_features, tile_values, tile_coords, tile_counts, first_weight, second_weight, out_grad
):
    node_rows = node_features.shape[0]
    edge = tile_values.shape[-1]
    slots = tile_values.shape[2]
    grid_rows = lax.axis_size("row")
    grid_cols = lax.axis_size("col")
    chips = grid_rows // 2
    per_node = node_rows // edge

    def gather_col(value):
        return jnp.concatenate(
            [value] + [swap(value, "col", k) for k in range(1, grid_cols)], axis=0
        )

    gathered_x = gather_col(node_features)
    dense = assemble(
        tile_values.reshape(slots, edge, edge),
        tile_coords.reshape(slots, 2).T,
        tile_counts.reshape(1),
        grid_rows * node_rows,
        grid_cols * node_rows,
        per_node,
    )
    dense_own, dense_other = dense[0], dense[1]
    grad_own = jnp.concatenate(
        [out_grad] + [swap(out_grad, "row", 2 * i) for i in range(1, chips)], axis=0
    )

    def chip_blocks(source):
        other = dot_parts(dense_other, source).astype(BF16)
        arrived = swap(other, "row", 1)
        chip_sum = dot_parts(dense_own, source) + arrived.astype(F32)
        return chip_sum.reshape(chips, node_rows, -1)

    def plane_sum(blocks):
        return tree_sum(
            [blocks[0]]
            + [swap(blocks[i].astype(BF16), "row", 2 * i) for i in range(1, chips)]
        )

    gathered_x, grad_own = lax.optimization_barrier((gathered_x, grad_own))
    grad_other = swap(grad_own, "row", 1)
    first_blocks = chip_blocks(gathered_x)

    first_blocks, grad_own, grad_other = lax.optimization_barrier(
        (first_blocks, grad_own, grad_other)
    )
    first_mean = plane_sum(first_blocks)
    back_part = dot_parts(dense_own, grad_own, 0) + dot_parts(dense_other, grad_other, 0)
    back_blocks = back_part.reshape(grid_cols, node_rows, -1)
    back_arrived = [swap(back_blocks[k].astype(BF16), "col", k) for k in range(1, grid_cols)]

    first_pre = dot_parts(first_mean, first_weight)
    projected = dot_parts(first_pre * jax.nn.sigmoid(first_pre), second_weight).astype(BF16)
    output = plane_sum(chip_blocks(gather_col(projected))).astype(BF16)

    scale = 1.0 / math.sqrt(node_rows * grid_rows * grid_cols)
    mine, theirs = local_grads(
        first_mean, first_pre, back_part, back_arrived, second_weight, scale
    )
    mine = (mine + swap(theirs, "row", 1).astype(F32)).astype(BF16)
    mine = tree_sum([mine] + [swap(mine, "row", 2 * i) for i in range(1, chips)]).astype(BF16)
    mine = tree_sum([mine] + [swap(mine, "col", k) for k in range(1, grid_cols)])
    first_grad, second_grad = join(mine, swap(mine, "row", 1), first_weight.shape[1])
    return (output, first_grad, second_grad)


def solution(mesh):
    return jax.shard_map(
        on_device,
        mesh=mesh,
        in_specs=(
            P(("row", "col"), None),
            P("row", "col", None, None, None),
            P("row", "col", None, None),
            P("row", "col"),
            P(),
            P(),
            P(("row", "col"), None),
        ),
        out_specs=(P(("row", "col"), None), P(), P()),
        check_vma=False,
    )
```

```python
import math

import jax
import jax.numpy as jnp
from jax import lax
from jax.experimental import pallas as pl
from jax.experimental.pallas import tpu as pltpu
from jax.sharding import PartitionSpec as P

BF16 = jnp.bfloat16
F32 = jnp.float32


def dot_parts(left, right, left_dim=1, right_dim=0):
    def parts(value):
        if value.dtype == BF16:
            return [value]
        high = lax.reduce_precision(value, 8, 7)
        return [high.astype(BF16), (value - high).astype(BF16)]

    lefts, rights = parts(left), parts(right)
    total = None
    for i, one in enumerate(lefts):
        for j, other in enumerate(rights):
            if i + j < 2:
                term = lax.dot_general(
                    one, other, (((left_dim,), (right_dim,)), ((), ())), preferred_element_type=F32
                )
                total = term if total is None else total + term
    return total


def tree_sum(parts):
    parts = [part.astype(F32) for part in parts]
    while len(parts) > 1:
        parts = [parts[i] + parts[i + 1] for i in range(0, len(parts), 2)]
    return parts[0]


def assemble_kernel(per_node, coords_ref, count_ref, tiles_ref, dense_ref, sem):
    slots, edge = tiles_ref.shape[0], tiles_ref.shape[1]
    halves, rows, cols = dense_ref.shape
    me_row, me_col = lax.axis_index("row"), lax.axis_index("col")
    live = count_ref[0]
    strip = math.gcd(rows, 256)
    shift = per_node.bit_length() - 1
    far_bit = lax.axis_size("col") // 2

    @pl.when(live * edge * edge < halves * rows * cols)
    def _():
        def clear(step, carry):
            place = pl.ds(pl.multiple_of(step * strip, strip), strip)
            for half in range(halves):
                dense_ref[half, place, :] = jnp.zeros((strip, cols), BF16)
            return carry

        lax.fori_loop(0, rows // strip, clear, 0)

    def begin(slot):
        row, col = coords_ref[0, slot], coords_ref[1, slot]
        offset = (row >> shift) ^ me_row
        row_place = ((offset >> 1) << shift) + (row & (per_node - 1))
        col_place = (((col >> shift) ^ me_col ^ far_bit) << shift) + (col & (per_node - 1))
        pltpu.make_async_copy(
            tiles_ref.at[slot],
            dense_ref.at[
                offset & 1,
                pl.ds(pl.multiple_of(row_place * edge, edge), edge),
                pl.ds(pl.multiple_of(col_place * edge, edge), edge),
            ],
            sem,
        ).start()

    def begin_group(step, carry):
        for i in range(8):
            begin(step * 8 + i)
        return carry

    def begin_one(slot, carry):
        begin(slot)
        return carry

    groups = live >> 3
    lax.fori_loop(0, groups, begin_group, 0)
    lax.fori_loop(groups << 3, live, begin_one, 0)
    size = 1
    while size <= slots:

        @pl.when((live & size) != 0)
        def _(size=size):
            some = tiles_ref.at[pl.ds(0, size)]
            pltpu.make_async_copy(some, some, sem).wait()

        size *= 2


def assemble(tiles, coords, count, rows, cols, per_node):
    def kernel(*refs):
        assemble_kernel(per_node, *refs)

    return pl.pallas_call(
        kernel,
        out_shape=jax.ShapeDtypeStruct((2, rows // 2, cols), BF16),
        in_specs=[
            pl.BlockSpec(memory_space=pltpu.SMEM),
            pl.BlockSpec(memory_space=pltpu.SMEM),
            pl.BlockSpec(memory_space=pltpu.HBM),
        ],
        out_specs=pl.BlockSpec(memory_space=pltpu.VMEM),
        scratch_shapes=[pltpu.SemaphoreType.DMA],
        compiler_params=pltpu.CompilerParams(vmem_limit_bytes=rows * cols * 2 + (2 << 20)),
        cost_estimate=pl.CostEstimate(
            flops=0, bytes_accessed=2 * rows * cols * 2, transcendentals=0
        ),
        name="assemble",
    )(coords, count, tiles)


def local_grads_kernel(scale, grid_cols, *refs):
    mean_ref, pre_ref, back_ref = refs[:3]
    arrived_refs = refs[3 : 2 + grid_cols]
    weight_ref, mine_ref, theirs_ref = refs[2 + grid_cols :]
    own = pl.ds(grid_cols // 2 * mean_ref.shape[0], mean_ref.shape[0])
    back_sum = tree_sum([back_ref[own, :]] + [ref[...] for ref in arrived_refs])
    hidden_grad = dot_parts(back_sum, weight_ref[...], 1, 1)
    first_pre = pre_ref[...]
    sigma = jax.nn.sigmoid(first_pre)
    hidden_act = (first_pre * sigma).astype(BF16)
    pre_grad = hidden_grad * (sigma * (1.0 + first_pre * (1.0 - sigma)))
    first = dot_parts(mean_ref[...], pre_grad, 0, 0) * scale
    second = dot_parts(hidden_act, back_sum, 0, 0) * scale
    half, width = mine_ref.shape[0], first.shape[1]
    low_core = lax.axis_index("row") % 2 == 0
    for value, place in ((first, slice(0, width)), (second, slice(width, None))):
        low, high = value[:half], value[half:]
        mine_ref[:, place] = jnp.where(low_core, low, high)
        theirs_ref[:, place] = jnp.where(low_core, high, low).astype(BF16)


def local_grads(mean, pre, back, arrived, weight, scale):
    grid_cols = len(arrived) + 1
    half = mean.shape[1] // 2
    width = pre.shape[1] + weight.shape[1]

    def kernel(*refs):
        local_grads_kernel(scale, grid_cols, *refs)

    vmem = pl.BlockSpec(memory_space=pltpu.VMEM)
    return pl.pallas_call(
        kernel,
        out_shape=(
            jax.ShapeDtypeStruct((half, width), F32),
            jax.ShapeDtypeStruct((half, width), BF16),
        ),
        in_specs=[vmem] * (4 + len(arrived)),
        out_specs=(vmem, vmem),
        compiler_params=pltpu.CompilerParams(vmem_limit_bytes=6 << 20),
        cost_estimate=pl.CostEstimate(
            flops=2 * 256 * 256 * 384 * 3, bytes_accessed=1 << 20, transcendentals=1 << 16
        ),
        name="local_grads",
    )(mean, pre, back, *arrived, weight)


def join_kernel(mine_ref, theirs_ref, first_ref, second_ref):
    half, width = mine_ref.shape[0], first_ref.shape[1]
    low_core = lax.axis_index("row") % 2 == 0
    for ref, place in ((first_ref, slice(0, width)), (second_ref, slice(width, None))):
        mine, theirs = mine_ref[:, place], theirs_ref[:, place]
        ref[:half, :] = jnp.where(low_core, mine, theirs)
        ref[half:, :] = jnp.where(low_core, theirs, mine)


def join(mine, theirs, width):
    vmem = pl.BlockSpec(memory_space=pltpu.VMEM)
    rows = 2 * mine.shape[0]
    return pl.pallas_call(
        join_kernel,
        out_shape=(
            jax.ShapeDtypeStruct((rows, width), F32),
            jax.ShapeDtypeStruct((rows, mine.shape[1] - width), F32),
        ),
        in_specs=[vmem, vmem],
        out_specs=(vmem, vmem),
        compiler_params=pltpu.CompilerParams(vmem_limit_bytes=2 << 20),
        name="join_grads",
    )(mine, theirs)


def swap(value, axis, offset):
    size = lax.axis_size(axis)
    return lax.ppermute(value, axis, [(i, i ^ offset) for i in range(size)])


def exchange(values, axis, stride, near=False):
    half = 0 if near else len(values) // 2
    arrived = [
        values[0] if k == 0 else swap(values[k], axis, k * stride)
        for k in (i ^ half for i in range(len(values)))
    ]
    return arrived


def on_device(
    node_features, tile_values, tile_coords, tile_counts, first_weight, second_weight, out_grad
):
    node_rows = node_features.shape[0]
    edge = tile_values.shape[-1]
    slots = tile_values.shape[2]
    grid_rows = lax.axis_size("row")
    grid_cols = lax.axis_size("col")
    chips = grid_rows // 2
    per_node = node_rows // edge

    def gather_col(value):
        return exchange([value] * grid_cols, "col", 1)

    parts_x = gather_col(node_features)
    gathered_x = jnp.concatenate(parts_x, axis=0)
    dense = assemble(
        tile_values.reshape(slots, edge, edge),
        tile_coords.reshape(slots, 2).T,
        tile_counts.reshape(1),
        grid_rows * node_rows,
        grid_cols * node_rows,
        per_node,
    )
    dense_own, dense_other = dense[0], dense[1]
    grad_own, offset = out_grad, 2
    while offset < grid_rows:
        grad_own = jnp.concatenate([grad_own, swap(grad_own, "row", offset)], axis=0)
        offset *= 2

    def chip_blocks(source):
        other = dot_parts(dense_other, source).astype(BF16)
        arrived = swap(other, "row", 1)
        own, arrived = lax.optimization_barrier((dot_parts(dense_own, source), arrived))
        return (own + arrived.astype(F32)).reshape(chips, node_rows, -1)

    def plane_sum(blocks, near):
        sent = [blocks[0]] + [blocks[i].astype(BF16) for i in range(1, chips)]
        return tree_sum(exchange(sent, "row", 2, near))

    gathered_x, grad_own = lax.optimization_barrier((gathered_x, grad_own))
    grad_other = swap(grad_own, "row", 1)
    first_blocks = chip_blocks(gathered_x)

    first_blocks, grad_own, grad_other = lax.optimization_barrier(
        (first_blocks, grad_own, grad_other)
    )
    first_mean = plane_sum(first_blocks, False)
    back_part = dot_parts(dense_own, grad_own, 0) + dot_parts(dense_other, grad_other, 0)
    back_blocks = back_part.reshape(grid_cols, node_rows, -1)
    back_sent = [back_blocks[i ^ (grid_cols // 2)] for i in range(grid_cols)]
    back_sent = [back_sent[0]] + [block.astype(BF16) for block in back_sent[1:]]
    back_arrived = exchange(back_sent, "col", 1, False)
    back_arrived.pop(grid_cols // 2)

    first_pre = dot_parts(first_mean, first_weight)
    projected = dot_parts(first_pre * jax.nn.sigmoid(first_pre), second_weight).astype(BF16)
    projected, first_pre = lax.optimization_barrier((projected, first_pre))
    parts_h = exchange([projected] * grid_cols, "col", 1, True)

    scale = 1.0 / math.sqrt(node_rows * grid_rows * grid_cols)
    mine, theirs = local_grads(
        first_mean, first_pre, back_part, back_arrived, second_weight, scale
    )
    mine = (mine + swap(theirs, "row", 1).astype(F32)).astype(BF16)
    _, *parts_h = lax.optimization_barrier((mine, *parts_h))
    parts_h = lax.optimization_barrier(parts_h)
    parts_h = [parts_h[i ^ (grid_cols // 2)] for i in range(grid_cols)]
    output = plane_sum(chip_blocks(jnp.concatenate(parts_h, axis=0)), False).astype(BF16)
    mine = tree_sum(exchange([mine] * chips, "row", 2, False)).astype(BF16)
    mine = tree_sum(exchange([mine] * grid_cols, "col", 1, True))
    first_grad, second_grad = join(mine, swap(mine, "row", 1), first_weight.shape[1])
    return (output, first_grad, second_grad)


def solution(mesh):
    return jax.shard_map(
        on_device,
        mesh=mesh,
        in_specs=(
            P(("row", "col"), None),
            P("row", "col", None, None, None),
            P("row", "col", None, None),
            P("row", "col"),
            P(),
            P(),
            P(("row", "col"), None),
        ),
        out_specs=(P(("row", "col"), None), P(), P()),
        check_vma=False,
    )
```

```python
import math

import jax
import jax.numpy as jnp
from jax import lax
from jax.experimental import pallas as pl
from jax.experimental.pallas import tpu as pltpu
from jax.sharding import PartitionSpec as P

BF16 = jnp.bfloat16
F32 = jnp.float32


def dot_parts(left, right, left_dim=1, right_dim=0):
    def parts(value):
        if value.dtype == BF16:
            return [value]
        high = lax.reduce_precision(value, 8, 7)
        return [high.astype(BF16), (value - high).astype(BF16)]

    lefts, rights = parts(left), parts(right)
    total = None
    for i, one in enumerate(lefts):
        for j, other in enumerate(rights):
            if i + j < 2:
                term = lax.dot_general(
                    one, other, (((left_dim,), (right_dim,)), ((), ())), preferred_element_type=F32
                )
                total = term if total is None else total + term
    return total


def tree_sum(parts):
    parts = [part.astype(F32) for part in parts]
    while len(parts) > 1:
        parts = [parts[i] + parts[i + 1] for i in range(0, len(parts), 2)]
    return parts[0]


def assemble_kernel(per_node, coords_ref, count_ref, tiles_ref, dense_ref, sem):
    slots, edge = tiles_ref.shape[0], tiles_ref.shape[1]
    halves, rows, cols = dense_ref.shape
    me_row, me_col = lax.axis_index("row"), lax.axis_index("col")
    live = count_ref[0]
    strip = math.gcd(rows, 256)
    shift = per_node.bit_length() - 1
    far_bit = lax.axis_size("col") - 1

    @pl.when(live * edge * edge < halves * rows * cols)
    def _():
        def clear(step, carry):
            place = pl.ds(pl.multiple_of(step * strip, strip), strip)
            for half in range(halves):
                dense_ref[half, place, :] = jnp.zeros((strip, cols), BF16)
            return carry

        lax.fori_loop(0, rows // strip, clear, 0)

    def begin(slot):
        row, col = coords_ref[0, slot], coords_ref[1, slot]
        offset = (row >> shift) ^ me_row
        row_place = ((offset >> 1) << shift) + (row & (per_node - 1))
        col_place = (((col >> shift) ^ me_col ^ far_bit) << shift) + (col & (per_node - 1))
        pltpu.make_async_copy(
            tiles_ref.at[slot],
            dense_ref.at[
                offset & 1,
                pl.ds(pl.multiple_of(row_place * edge, edge), edge),
                pl.ds(pl.multiple_of(col_place * edge, edge), edge),
            ],
            sem,
        ).start()

    def begin_group(step, carry):
        for i in range(8):
            begin(step * 8 + i)
        return carry

    def begin_one(slot, carry):
        begin(slot)
        return carry

    groups = live >> 3
    lax.fori_loop(0, groups, begin_group, 0)
    lax.fori_loop(groups << 3, live, begin_one, 0)
    size = 1
    while size <= slots:

        @pl.when((live & size) != 0)
        def _(size=size):
            some = tiles_ref.at[pl.ds(0, size)]
            pltpu.make_async_copy(some, some, sem).wait()

        size *= 2


def assemble(tiles, coords, count, rows, cols, per_node):
    def kernel(*refs):
        assemble_kernel(per_node, *refs)

    return pl.pallas_call(
        kernel,
        out_shape=jax.ShapeDtypeStruct((2, rows // 2, cols), BF16),
        in_specs=[
            pl.BlockSpec(memory_space=pltpu.SMEM),
            pl.BlockSpec(memory_space=pltpu.SMEM),
            pl.BlockSpec(memory_space=pltpu.HBM),
        ],
        out_specs=pl.BlockSpec(memory_space=pltpu.VMEM),
        scratch_shapes=[pltpu.SemaphoreType.DMA],
        compiler_params=pltpu.CompilerParams(vmem_limit_bytes=max(47 << 20, rows * cols * 2 + (2 << 20))),
        cost_estimate=pl.CostEstimate(
            flops=0, bytes_accessed=2 * rows * cols * 2, transcendentals=0
        ),
        name="assemble",
    )(coords, count, tiles)


def local_grads_kernel(scale, grid_cols, *refs):
    mean_ref, pre_ref, back_ref = refs[:3]
    arrived_refs = refs[3 : 2 + grid_cols]
    weight_ref, mine_ref, theirs_ref = refs[2 + grid_cols :]
    own = pl.ds((grid_cols - 1) * mean_ref.shape[0], mean_ref.shape[0])
    back_sum = tree_sum([back_ref[own, :]] + [ref[...] for ref in arrived_refs])
    hidden_grad = dot_parts(back_sum, weight_ref[...], 1, 1)
    first_pre = pre_ref[...]
    sigma = jax.nn.sigmoid(first_pre)
    hidden_act = (first_pre * sigma).astype(BF16)
    pre_grad = hidden_grad * (sigma * (1.0 + first_pre * (1.0 - sigma)))
    first = dot_parts(mean_ref[...], pre_grad, 0, 0) * scale
    second = dot_parts(hidden_act, back_sum, 0, 0) * scale
    half, width = mine_ref.shape[0], first.shape[1]
    low_core = lax.axis_index("row") % 2 == 0
    for value, place in ((first, slice(0, width)), (second, slice(width, None))):
        low, high = value[:half], value[half:]
        mine_ref[:, place] = jnp.where(low_core, low, high)
        theirs_ref[:, place] = jnp.where(low_core, high, low).astype(BF16)


def local_grads(mean, pre, back, arrived, weight, scale):
    grid_cols = len(arrived) + 1
    half = mean.shape[1] // 2
    width = pre.shape[1] + weight.shape[1]

    def kernel(*refs):
        local_grads_kernel(scale, grid_cols, *refs)

    vmem = pl.BlockSpec(memory_space=pltpu.VMEM)
    return pl.pallas_call(
        kernel,
        out_shape=(
            jax.ShapeDtypeStruct((half, width), F32),
            jax.ShapeDtypeStruct((half, width), BF16),
        ),
        in_specs=[vmem] * (4 + len(arrived)),
        out_specs=(vmem, vmem),
        compiler_params=pltpu.CompilerParams(vmem_limit_bytes=6 << 20),
        cost_estimate=pl.CostEstimate(
            flops=2 * 256 * 256 * 384 * 3, bytes_accessed=1 << 20, transcendentals=1 << 16
        ),
        name="local_grads",
    )(mean, pre, back, *arrived, weight)


def join_kernel(mine_ref, theirs_ref, first_ref, second_ref):
    half, width = mine_ref.shape[0], first_ref.shape[1]
    low_core = lax.axis_index("row") % 2 == 0
    for ref, place in ((first_ref, slice(0, width)), (second_ref, slice(width, None))):
        mine, theirs = mine_ref[:, place], theirs_ref[:, place]
        ref[:half, :] = jnp.where(low_core, mine, theirs)
        ref[half:, :] = jnp.where(low_core, theirs, mine)


def join(mine, theirs, width):
    vmem = pl.BlockSpec(memory_space=pltpu.VMEM)
    rows = 2 * mine.shape[0]
    return pl.pallas_call(
        join_kernel,
        out_shape=(
            jax.ShapeDtypeStruct((rows, width), F32),
            jax.ShapeDtypeStruct((rows, mine.shape[1] - width), F32),
        ),
        in_specs=[vmem, vmem],
        out_specs=(vmem, vmem),
        compiler_params=pltpu.CompilerParams(vmem_limit_bytes=2 << 20),
        name="join_grads",
    )(mine, theirs)


def activate_kernel(chips, flip, *refs):
    blocks_ref, arrived_refs = refs[0], refs[1:chips]
    first_ref, second_ref, mean_ref, pre_ref, projected_ref = refs[chips:]
    parts = [ref[...] for ref in arrived_refs]
    parts.insert(flip, blocks_ref[0])
    mean = tree_sum(parts)
    pre = dot_parts(mean, first_ref[...])
    mean_ref[...] = mean
    pre_ref[...] = pre
    projected_ref[...] = dot_parts(pre * jax.nn.sigmoid(pre), second_ref[...]).astype(BF16)


def activate(blocks, parts, flip, first_weight, second_weight):
    chips, rows, _ = blocks.shape
    arrived = parts[:flip] + parts[flip + 1 :]

    def kernel(*refs):
        activate_kernel(chips, flip, *refs)

    vmem = pl.BlockSpec(memory_space=pltpu.VMEM)
    return pl.pallas_call(
        kernel,
        out_shape=(
            jax.ShapeDtypeStruct((rows, first_weight.shape[0]), F32),
            jax.ShapeDtypeStruct((rows, first_weight.shape[1]), F32),
            jax.ShapeDtypeStruct((rows, second_weight.shape[1]), BF16),
        ),
        in_specs=[vmem] * (chips + 2),
        out_specs=(vmem, vmem, vmem),
        compiler_params=pltpu.CompilerParams(vmem_limit_bytes=6 << 20),
        name="activate",
    )(blocks, *arrived, first_weight, second_weight)


def swap(value, axis, offset):
    size = lax.axis_size(axis)
    return lax.ppermute(value, axis, [(i, i ^ offset) for i in range(size)])


def exchange(values, axis, stride, flip):
    arrived = {}
    for i in range(len(values)):
        k = i ^ flip
        arrived[k] = swap(values[k], axis, k * stride) if k else values[0]
    return [arrived[k] for k in range(len(values))]


def in_order(values, flip):
    return [values[i ^ flip] for i in range(len(values))]


def tree_in_order(values, flip):
    return tree_sum(in_order(values, flip))


def on_device(
    node_features, tile_values, tile_coords, tile_counts, first_weight, second_weight, out_grad
):
    node_rows = node_features.shape[0]
    edge = tile_values.shape[-1]
    slots = tile_values.shape[2]
    grid_rows = lax.axis_size("row")
    grid_cols = lax.axis_size("col")
    chips = grid_rows // 2
    per_node = node_rows // edge
    far = grid_cols - 1

    features = exchange([node_features] * grid_cols, "col", 1, far)
    gathered_x = jnp.concatenate(in_order(features, far), axis=0)
    dense = assemble(
        tile_values.reshape(slots, edge, edge),
        tile_coords.reshape(slots, 2).T,
        tile_counts.reshape(1),
        grid_rows * node_rows,
        grid_cols * node_rows,
        per_node,
    )
    dense_own, dense_other = dense[0], dense[1]
    grad_own, offset = out_grad, 2
    while offset < grid_rows:
        grad_own = jnp.concatenate([grad_own, swap(grad_own, "row", offset)], axis=0)
        offset *= 2
    partner = dot_parts(dense_other, gathered_x).astype(BF16)
    back_own = dot_parts(dense_own, grad_own, 0)
    arrived = swap(partner, "row", 1)
    own, arrived = lax.optimization_barrier((dot_parts(dense_own, gathered_x), arrived))
    first_blocks = (own + arrived.astype(F32)).reshape(chips, node_rows, -1)
    grad_other = swap(grad_own, "row", 1)
    back_part = back_own + dot_parts(dense_other, grad_other, 0)
    first_blocks, back_part = lax.optimization_barrier((first_blocks, back_part))
    first_sent = [first_blocks[0]] + [block.astype(BF16) for block in first_blocks[1:]]
    back_blocks = back_part.reshape(grid_cols, node_rows, -1)
    back_sent = [back_blocks[k ^ far] for k in range(grid_cols)]
    back_sent = [back_sent[0]] + [block.astype(BF16) for block in back_sent[1:]]
    first_parts = exchange(first_sent, "row", 2, chips - 1)
    back_arrived = in_order(exchange(back_sent, "col", 1, grid_cols // 2), grid_cols // 2)
    back_arrived.pop(grid_cols // 2)
    first_mean, first_pre, projected = activate(
        first_blocks, in_order(first_parts, chips - 1), chips - 1, first_weight, second_weight
    )
    projected, first_pre = lax.optimization_barrier((projected, first_pre))
    parts_h = exchange([projected] * grid_cols, "col", 1, grid_cols - 1)

    scale = 1.0 / math.sqrt(node_rows * grid_rows * grid_cols)
    mine, theirs = local_grads(
        first_mean, first_pre, back_part, back_arrived, second_weight, scale
    )
    mine = (mine + swap(theirs, "row", 1).astype(F32)).astype(BF16)
    _, *parts_h = lax.optimization_barrier((mine, *parts_h))
    parts_h = in_order(lax.optimization_barrier(in_order(parts_h, grid_cols - 1)), grid_cols - 1)
    gathered_h = jnp.concatenate(in_order(parts_h, far), axis=0)
    partner = dot_parts(dense_other, gathered_h).astype(BF16)
    arrived = swap(partner, "row", 1)
    own, arrived = lax.optimization_barrier((dot_parts(dense_own, gathered_h), arrived))
    blocks = (own + arrived.astype(F32)).reshape(chips, node_rows, -1)
    mine = tree_in_order(exchange([mine] * chips, "row", 2, 0), 0).astype(BF16)
    sent = [blocks[0]] + [block.astype(BF16) for block in blocks[1:]]
    output = tree_in_order(exchange(sent, "row", 2, chips // 2), chips // 2).astype(BF16)
    mine = tree_in_order(exchange([mine] * grid_cols, "col", 1, 0), 0)
    first_grad, second_grad = join(mine, swap(mine, "row", 1), first_weight.shape[1])
    return (output, first_grad, second_grad)


def solution(mesh):
    return jax.shard_map(
        on_device,
        mesh=mesh,
        in_specs=(
            P(("row", "col"), None),
            P("row", "col", None, None, None),
            P("row", "col", None, None),
            P("row", "col"),
            P(),
            P(),
            P(("row", "col"), None),
        ),
        out_specs=(P(("row", "col"), None), P(), P()),
        check_vma=False,
    )
```

```python
import math

import jax
import jax.numpy as jnp
from jax import lax
from jax.experimental import pallas as pl
from jax.experimental.pallas import tpu as pltpu
from jax.sharding import PartitionSpec as P

BF16 = jnp.bfloat16
F32 = jnp.float32


def dot_parts(left, right, left_dim=1, right_dim=0):
    def parts(value):
        if value.dtype == BF16:
            return [value]
        high = lax.reduce_precision(value, 8, 7)
        return [high.astype(BF16), (value - high).astype(BF16)]

    lefts, rights = parts(left), parts(right)
    total = None
    for i, one in enumerate(lefts):
        for j, other in enumerate(rights):
            if i + j < 2:
                term = lax.dot_general(
                    one, other, (((left_dim,), (right_dim,)), ((), ())), preferred_element_type=F32
                )
                total = term if total is None else total + term
    return total


def tree_sum(parts):
    parts = [part.astype(F32) for part in parts]
    while len(parts) > 1:
        parts = [parts[i] + parts[i + 1] for i in range(0, len(parts), 2)]
    return parts[0]


def assemble_kernel(per_node, coords_ref, count_ref, tiles_ref, dense_ref, sem):
    slots, edge = tiles_ref.shape[0], tiles_ref.shape[1]
    halves, rows, cols = dense_ref.shape
    me_row, me_col = lax.axis_index("row"), lax.axis_index("col")
    live = count_ref[0]
    strip = math.gcd(rows, 256)
    shift = per_node.bit_length() - 1
    far_bit = lax.axis_size("col") - 1

    @pl.when(live * edge * edge < halves * rows * cols)
    def _():
        def clear(step, carry):
            place = pl.ds(pl.multiple_of(step * strip, strip), strip)
            for half in range(halves):
                dense_ref[half, place, :] = jnp.zeros((strip, cols), BF16)
            return carry

        lax.fori_loop(0, rows // strip, clear, 0)

    def begin(slot):
        row, col = coords_ref[0, slot], coords_ref[1, slot]
        offset = (row >> shift) ^ me_row
        row_place = ((offset >> 1) << shift) + (row & (per_node - 1))
        col_place = (((col >> shift) ^ me_col ^ far_bit) << shift) + (col & (per_node - 1))
        pltpu.make_async_copy(
            tiles_ref.at[slot],
            dense_ref.at[
                offset & 1,
                pl.ds(pl.multiple_of(row_place * edge, edge), edge),
                pl.ds(pl.multiple_of(col_place * edge, edge), edge),
            ],
            sem,
        ).start()

    def begin_group(step, carry):
        for i in range(8):
            begin(step * 8 + i)
        return carry

    def begin_one(slot, carry):
        begin(slot)
        return carry

    groups = live >> 3
    lax.fori_loop(0, groups, begin_group, 0)
    lax.fori_loop(groups << 3, live, begin_one, 0)
    size = 1
    while size <= slots:

        @pl.when((live & size) != 0)
        def _(size=size):
            some = tiles_ref.at[pl.ds(0, size)]
            pltpu.make_async_copy(some, some, sem).wait()

        size *= 2


def assemble(tiles, coords, count, rows, cols, per_node):
    def kernel(*refs):
        assemble_kernel(per_node, *refs)

    return pl.pallas_call(
        kernel,
        out_shape=jax.ShapeDtypeStruct((2, rows // 2, cols), BF16),
        in_specs=[
            pl.BlockSpec(memory_space=pltpu.SMEM),
            pl.BlockSpec(memory_space=pltpu.SMEM),
            pl.BlockSpec(memory_space=pltpu.HBM),
        ],
        out_specs=pl.BlockSpec(memory_space=pltpu.VMEM),
        scratch_shapes=[pltpu.SemaphoreType.DMA],
        compiler_params=pltpu.CompilerParams(vmem_limit_bytes=max(47 << 20, rows * cols * 2 + (2 << 20))),
        cost_estimate=pl.CostEstimate(
            flops=0, bytes_accessed=2 * rows * cols * 2, transcendentals=0
        ),
        name="assemble",
    )(coords, count, tiles)


def local_grads_kernel(scale, grid_cols, *refs):
    mean_ref, pre_ref, back_ref = refs[:3]
    arrived_refs = refs[3 : 2 + grid_cols]
    weight_ref, mine_ref, theirs_ref = refs[2 + grid_cols :]
    own = pl.ds((grid_cols - 1) * mean_ref.shape[0], mean_ref.shape[0])
    back_sum = tree_sum([back_ref[own, :]] + [ref[...] for ref in arrived_refs])
    hidden_grad = dot_parts(back_sum, weight_ref[...], 1, 1)
    first_pre = pre_ref[...]
    sigma = jax.nn.sigmoid(first_pre)
    hidden_act = (first_pre * sigma).astype(BF16)
    pre_grad = hidden_grad * (sigma * (1.0 + first_pre * (1.0 - sigma)))
    first = dot_parts(mean_ref[...], pre_grad, 0, 0) * scale
    second = dot_parts(hidden_act, back_sum, 0, 0) * scale
    half, width = mine_ref.shape[0], first.shape[1]
    low_core = lax.axis_index("row") % 2 == 0
    for value, place in ((first, slice(0, width)), (second, slice(width, None))):
        low, high = value[:half], value[half:]
        mine_ref[:, place] = jnp.where(low_core, low, high)
        theirs_ref[:, place] = jnp.where(low_core, high, low).astype(BF16)


def local_grads(mean, pre, back, arrived, weight, scale):
    grid_cols = len(arrived) + 1
    half = mean.shape[1] // 2
    width = pre.shape[1] + weight.shape[1]

    def kernel(*refs):
        local_grads_kernel(scale, grid_cols, *refs)

    vmem = pl.BlockSpec(memory_space=pltpu.VMEM)
    return pl.pallas_call(
        kernel,
        out_shape=(
            jax.ShapeDtypeStruct((half, width), F32),
            jax.ShapeDtypeStruct((half, width), BF16),
        ),
        in_specs=[vmem] * (4 + len(arrived)),
        out_specs=(vmem, vmem),
        compiler_params=pltpu.CompilerParams(vmem_limit_bytes=6 << 20),
        cost_estimate=pl.CostEstimate(
            flops=2 * 256 * 256 * 384 * 3, bytes_accessed=1 << 20, transcendentals=1 << 16
        ),
        name="local_grads",
    )(mean, pre, back, *arrived, weight)


def join_kernel(mine_ref, theirs_ref, first_ref, second_ref):
    half, width = mine_ref.shape[0], first_ref.shape[1]
    low_core = lax.axis_index("row") % 2 == 0
    for ref, place in ((first_ref, slice(0, width)), (second_ref, slice(width, None))):
        mine, theirs = mine_ref[:, place], theirs_ref[:, place]
        ref[:half, :] = jnp.where(low_core, mine, theirs)
        ref[half:, :] = jnp.where(low_core, theirs, mine)


def join(mine, theirs, width):
    vmem = pl.BlockSpec(memory_space=pltpu.VMEM)
    rows = 2 * mine.shape[0]
    return pl.pallas_call(
        join_kernel,
        out_shape=(
            jax.ShapeDtypeStruct((rows, width), F32),
            jax.ShapeDtypeStruct((rows, mine.shape[1] - width), F32),
        ),
        in_specs=[vmem, vmem],
        out_specs=(vmem, vmem),
        compiler_params=pltpu.CompilerParams(vmem_limit_bytes=2 << 20),
        name="join_grads",
    )(mine, theirs)


def activate_kernel(chips, flip, *refs):
    blocks_ref, arrived_refs = refs[0], refs[1:chips]
    first_ref, second_ref, mean_ref, pre_ref, projected_ref = refs[chips:]
    parts = [ref[...] for ref in arrived_refs]
    parts.insert(flip, blocks_ref[0])
    mean = tree_sum(parts)
    pre = dot_parts(mean, first_ref[...])
    mean_ref[...] = mean
    pre_ref[...] = pre
    projected_ref[...] = dot_parts(pre * jax.nn.sigmoid(pre), second_ref[...]).astype(BF16)


def activate(blocks, parts, flip, first_weight, second_weight):
    chips, rows, _ = blocks.shape
    arrived = parts[:flip] + parts[flip + 1 :]

    def kernel(*refs):
        activate_kernel(chips, flip, *refs)

    vmem = pl.BlockSpec(memory_space=pltpu.VMEM)
    return pl.pallas_call(
        kernel,
        out_shape=(
            jax.ShapeDtypeStruct((rows, first_weight.shape[0]), F32),
            jax.ShapeDtypeStruct((rows, first_weight.shape[1]), F32),
            jax.ShapeDtypeStruct((rows, second_weight.shape[1]), BF16),
        ),
        in_specs=[vmem] * (chips + 2),
        out_specs=(vmem, vmem, vmem),
        compiler_params=pltpu.CompilerParams(vmem_limit_bytes=6 << 20),
        name="activate",
    )(blocks, *arrived, first_weight, second_weight)


def swap(value, axis, offset):
    size = lax.axis_size(axis)
    return lax.ppermute(value, axis, [(i, i ^ offset) for i in range(size)])


def exchange(values, axis, stride, flip):
    arrived = {}
    for i in range(len(values)):
        k = i ^ flip
        arrived[k] = swap(values[k], axis, k * stride) if k else values[0]
    return [arrived[k] for k in range(len(values))]


def in_order(values, flip):
    return [values[i ^ flip] for i in range(len(values))]


def tree_in_order(values, flip):
    return tree_sum(in_order(values, flip))


def on_device(
    node_features, tile_values, tile_coords, tile_counts, first_weight, second_weight, out_grad
):
    node_rows = node_features.shape[0]
    edge = tile_values.shape[-1]
    slots = tile_values.shape[2]
    grid_rows = lax.axis_size("row")
    grid_cols = lax.axis_size("col")
    chips = grid_rows // 2
    per_node = node_rows // edge
    far = grid_cols - 1

    features = exchange([node_features] * grid_cols, "col", 1, far)
    gathered_x = jnp.concatenate(in_order(features, far), axis=0)
    dense = assemble(
        tile_values.reshape(slots, edge, edge),
        tile_coords.reshape(slots, 2).T,
        tile_counts.reshape(1),
        grid_rows * node_rows,
        grid_cols * node_rows,
        per_node,
    )
    dense_own, dense_other = dense[0], dense[1]
    grad_own, offset = out_grad, 2
    while offset < grid_rows:
        grad_own = jnp.concatenate([grad_own, swap(grad_own, "row", offset)], axis=0)
        offset *= 2
    partner = dot_parts(dense_other, gathered_x).astype(BF16)
    back_own = dot_parts(dense_own, grad_own, 0)
    arrived = swap(partner, "row", 1)
    own, arrived = lax.optimization_barrier((dot_parts(dense_own, gathered_x), arrived))
    first_blocks = (own + arrived.astype(F32)).reshape(chips, node_rows, -1)
    grad_other = swap(grad_own, "row", 1)
    back_part = back_own + dot_parts(dense_other, grad_other, 0)
    first_blocks, back_part = lax.optimization_barrier((first_blocks, back_part))
    first_sent = [first_blocks[0]] + [block.astype(BF16) for block in first_blocks[1:]]
    back_blocks = back_part.reshape(grid_cols, node_rows, -1)
    back_sent = [back_blocks[k ^ far] for k in range(grid_cols)]
    back_sent = [back_sent[0]] + [block.astype(BF16) for block in back_sent[1:]]
    first_parts = exchange(first_sent, "row", 2, chips - 1)
    back_arrived = in_order(exchange(back_sent, "col", 1, grid_cols // 2), grid_cols // 2)
    back_arrived.pop(grid_cols // 2)
    first_mean, first_pre, projected = activate(
        first_blocks, in_order(first_parts, chips - 1), chips - 1, first_weight, second_weight
    )
    projected, first_pre = lax.optimization_barrier((projected, first_pre))
    parts_h = exchange([projected] * grid_cols, "col", 1, grid_cols // 2)

    scale = 1.0 / math.sqrt(node_rows * grid_rows * grid_cols)
    mine, theirs = local_grads(
        first_mean, first_pre, back_part, back_arrived, second_weight, scale
    )
    mine = (mine + swap(theirs, "row", 1).astype(F32)).astype(BF16)
    _, *parts_h = lax.optimization_barrier((mine, *parts_h))
    parts_h = in_order(lax.optimization_barrier(in_order(parts_h, grid_cols // 2)), grid_cols // 2)
    gathered_h = jnp.concatenate(in_order(parts_h, far), axis=0)
    partner = dot_parts(dense_other, gathered_h).astype(BF16)
    arrived = swap(partner, "row", 1)
    own, arrived = lax.optimization_barrier((dot_parts(dense_own, gathered_h), arrived))
    blocks = (own + arrived.astype(F32)).reshape(chips, node_rows, -1)
    mine = tree_in_order(exchange([mine] * chips, "row", 2, chips - 1), chips - 1).astype(BF16)
    sent = [blocks[0]] + [block.astype(BF16) for block in blocks[1:]]
    output = tree_in_order(exchange(sent, "row", 2, chips // 2), chips // 2).astype(BF16)
    mine = tree_in_order(exchange([mine] * grid_cols, "col", 1, 0), 0)
    first_grad, second_grad = join(mine, swap(mine, "row", 1), first_weight.shape[1])
    return (output, first_grad, second_grad)


def solution(mesh):
    return jax.shard_map(
        on_device,
        mesh=mesh,
        in_specs=(
            P(("row", "col"), None),
            P("row", "col", None, None, None),
            P("row", "col", None, None),
            P("row", "col"),
            P(),
            P(),
            P(("row", "col"), None),
        ),
        out_specs=(P(("row", "col"), None), P(), P()),
        check_vma=False,
    )
```

```python
import math

import jax
import jax.numpy as jnp
from jax import lax
from jax.experimental import pallas as pl
from jax.experimental.pallas import tpu as pltpu
from jax.sharding import PartitionSpec as P

BF16 = jnp.bfloat16
F32 = jnp.float32


def dot_parts(left, right, left_dim=1, right_dim=0):
    def parts(value):
        if value.dtype == BF16:
            return [value]
        high = lax.reduce_precision(value, 8, 7)
        return [high.astype(BF16), (value - high).astype(BF16)]

    lefts, rights = parts(left), parts(right)
    total = None
    for i, one in enumerate(lefts):
        for j, other in enumerate(rights):
            if i + j < 2:
                term = lax.dot_general(
                    one, other, (((left_dim,), (right_dim,)), ((), ())), preferred_element_type=F32
                )
                total = term if total is None else total + term
    return total


def tree_sum(parts):
    parts = [part.astype(F32) for part in parts]
    while len(parts) > 1:
        parts = [parts[i] + parts[i + 1] for i in range(0, len(parts), 2)]
    return parts[0]


def assemble_kernel(per_node, coords_ref, count_ref, tiles_ref, dense_ref, sem):
    slots, edge = tiles_ref.shape[0], tiles_ref.shape[1]
    halves, rows, cols = dense_ref.shape
    me_row, me_col = lax.axis_index("row"), lax.axis_index("col")
    live = count_ref[0]
    strip = math.gcd(rows, 256)
    shift = per_node.bit_length() - 1
    far_bit = lax.axis_size("col") - 1

    @pl.when(live * edge * edge < halves * rows * cols)
    def _():
        def clear(step, carry):
            place = pl.ds(pl.multiple_of(step * strip, strip), strip)
            for half in range(halves):
                dense_ref[half, place, :] = jnp.zeros((strip, cols), BF16)
            return carry

        lax.fori_loop(0, rows // strip, clear, 0)

    def begin(slot):
        row, col = coords_ref[0, slot], coords_ref[1, slot]
        offset = (row >> shift) ^ me_row
        row_place = ((offset >> 1) << shift) + (row & (per_node - 1))
        col_place = (((col >> shift) ^ me_col ^ far_bit) << shift) + (col & (per_node - 1))
        pltpu.make_async_copy(
            tiles_ref.at[slot],
            dense_ref.at[
                offset & 1,
                pl.ds(pl.multiple_of(row_place * edge, edge), edge),
                pl.ds(pl.multiple_of(col_place * edge, edge), edge),
            ],
            sem,
        ).start()

    def begin_group(step, carry):
        for i in range(8):
            begin(step * 8 + i)
        return carry

    def begin_one(slot, carry):
        begin(slot)
        return carry

    groups = live >> 3
    lax.fori_loop(0, groups, begin_group, 0)
    lax.fori_loop(groups << 3, live, begin_one, 0)
    size = 1
    while size <= slots:

        @pl.when((live & size) != 0)
        def _(size=size):
            some = tiles_ref.at[pl.ds(0, size)]
            pltpu.make_async_copy(some, some, sem).wait()

        size *= 2


def assemble(tiles, coords, count, rows, cols, per_node):
    def kernel(*refs):
        assemble_kernel(per_node, *refs)

    return pl.pallas_call(
        kernel,
        out_shape=jax.ShapeDtypeStruct((2, rows // 2, cols), BF16),
        in_specs=[
            pl.BlockSpec(memory_space=pltpu.SMEM),
            pl.BlockSpec(memory_space=pltpu.SMEM),
            pl.BlockSpec(memory_space=pltpu.HBM),
        ],
        out_specs=pl.BlockSpec(memory_space=pltpu.VMEM),
        scratch_shapes=[pltpu.SemaphoreType.DMA],
        compiler_params=pltpu.CompilerParams(vmem_limit_bytes=max(47 << 20, rows * cols * 2 + (2 << 20))),
        cost_estimate=pl.CostEstimate(
            flops=0, bytes_accessed=2 * rows * cols * 2, transcendentals=0
        ),
        name="assemble",
    )(coords, count, tiles)


def local_grads_kernel(scale, grid_cols, *refs):
    mean_ref, act_ref, slope_ref, back_ref = refs[:4]
    arrived_refs = refs[4 : 3 + grid_cols]
    weight_ref, mine_ref, theirs_ref = refs[3 + grid_cols :]
    own = pl.ds((grid_cols - 1) * slope_ref.shape[0], slope_ref.shape[0])
    back_sum = tree_sum([back_ref[own, :]] + [ref[...] for ref in arrived_refs])
    hidden_grad = dot_parts(back_sum, weight_ref[...], 1, 1)
    first = dot_parts(mean_ref[...], hidden_grad * slope_ref[...]) * scale
    second = dot_parts(act_ref[...], back_sum) * scale
    half, width = mine_ref.shape[0], first.shape[1]
    low_core = lax.axis_index("row") % 2 == 0
    for value, place in ((first, slice(0, width)), (second, slice(width, None))):
        low, high = value[:half], value[half:]
        mine_ref[:, place] = jnp.where(low_core, low, high)
        theirs_ref[:, place] = jnp.where(low_core, high, low).astype(BF16)


def local_grads(mean, act, slope, back, arrived, weight, scale):
    grid_cols = len(arrived) + 1
    half = mean.shape[0] // 2
    width = slope.shape[1] + weight.shape[1]

    def kernel(*refs):
        local_grads_kernel(scale, grid_cols, *refs)

    vmem = pl.BlockSpec(memory_space=pltpu.VMEM)
    return pl.pallas_call(
        kernel,
        out_shape=(
            jax.ShapeDtypeStruct((half, width), F32),
            jax.ShapeDtypeStruct((half, width), BF16),
        ),
        in_specs=[vmem] * (5 + len(arrived)),
        out_specs=(vmem, vmem),
        compiler_params=pltpu.CompilerParams(vmem_limit_bytes=6 << 20),
        cost_estimate=pl.CostEstimate(
            flops=2 * 256 * 256 * 384 * 3, bytes_accessed=1 << 20, transcendentals=1 << 16
        ),
        name="local_grads",
    )(mean, act, slope, back, *arrived, weight)


def join_kernel(mine_ref, theirs_ref, first_ref, second_ref):
    half, width = mine_ref.shape[0], first_ref.shape[1]
    low_core = lax.axis_index("row") % 2 == 0
    for ref, place in ((first_ref, slice(0, width)), (second_ref, slice(width, None))):
        mine, theirs = mine_ref[:, place], theirs_ref[:, place]
        ref[:half, :] = jnp.where(low_core, mine, theirs)
        ref[half:, :] = jnp.where(low_core, theirs, mine)


def join(mine, theirs, width):
    vmem = pl.BlockSpec(memory_space=pltpu.VMEM)
    rows = 2 * mine.shape[0]
    return pl.pallas_call(
        join_kernel,
        out_shape=(
            jax.ShapeDtypeStruct((rows, width), F32),
            jax.ShapeDtypeStruct((rows, mine.shape[1] - width), F32),
        ),
        in_specs=[vmem, vmem],
        out_specs=(vmem, vmem),
        compiler_params=pltpu.CompilerParams(vmem_limit_bytes=2 << 20),
        name="join_grads",
    )(mine, theirs)


def activate_kernel(chips, flip, *refs):
    blocks_ref, arrived_refs = refs[0], refs[1:chips]
    first_ref, second_ref, mean_ref, act_ref, slope_ref, projected_ref = refs[chips:]
    parts = [ref[...] for ref in arrived_refs]
    parts.insert(flip, blocks_ref[0])
    mean = tree_sum(parts)
    pre = dot_parts(mean, first_ref[...])
    sigma = jax.nn.sigmoid(pre)
    act = pre * sigma
    projected_ref[...] = dot_parts(act, second_ref[...]).astype(BF16)
    mean_ref[...] = mean.T
    act_ref[...] = act.T.astype(BF16)
    slope_ref[...] = sigma * (1.0 + pre * (1.0 - sigma))


def activate(blocks, parts, flip, first_weight, second_weight):
    chips, rows, _ = blocks.shape
    arrived = parts[:flip] + parts[flip + 1 :]

    def kernel(*refs):
        activate_kernel(chips, flip, *refs)

    vmem = pl.BlockSpec(memory_space=pltpu.VMEM)
    return pl.pallas_call(
        kernel,
        out_shape=(
            jax.ShapeDtypeStruct((first_weight.shape[0], rows), F32),
            jax.ShapeDtypeStruct((first_weight.shape[1], rows), BF16),
            jax.ShapeDtypeStruct((rows, first_weight.shape[1]), F32),
            jax.ShapeDtypeStruct((rows, second_weight.shape[1]), BF16),
        ),
        in_specs=[vmem] * (chips + 2),
        out_specs=(vmem, vmem, vmem, vmem),
        compiler_params=pltpu.CompilerParams(vmem_limit_bytes=6 << 20),
        name="activate",
    )(blocks, *arrived, first_weight, second_weight)


def swap(value, axis, offset):
    size = lax.axis_size(axis)
    return lax.ppermute(value, axis, [(i, i ^ offset) for i in range(size)])


def exchange(values, axis, stride, flip):
    arrived = {}
    for i in range(len(values)):
        k = i ^ flip
        arrived[k] = swap(values[k], axis, k * stride) if k else values[0]
    return [arrived[k] for k in range(len(values))]


def in_order(values, flip):
    return [values[i ^ flip] for i in range(len(values))]


def tree_in_order(values, flip):
    return tree_sum(in_order(values, flip))


def on_device(
    node_features, tile_values, tile_coords, tile_counts, first_weight, second_weight, out_grad
):
    node_rows = node_features.shape[0]
    edge = tile_values.shape[-1]
    slots = tile_values.shape[2]
    grid_rows = lax.axis_size("row")
    grid_cols = lax.axis_size("col")
    chips = grid_rows // 2
    per_node = node_rows // edge
    far = grid_cols - 1

    features = exchange([node_features] * grid_cols, "col", 1, far)
    gathered_x = jnp.concatenate(in_order(features, far), axis=0)
    dense = assemble(
        tile_values.reshape(slots, edge, edge),
        tile_coords.reshape(slots, 2).T,
        tile_counts.reshape(1),
        grid_rows * node_rows,
        grid_cols * node_rows,
        per_node,
    )
    dense_own, dense_other = dense[0], dense[1]
    grad_own, offset = out_grad, 2
    while offset < grid_rows:
        grad_own = jnp.concatenate([grad_own, swap(grad_own, "row", offset)], axis=0)
        offset *= 2
    partner = dot_parts(dense_other, gathered_x).astype(BF16)
    back_own = dot_parts(dense_own, grad_own, 0)
    arrived = swap(partner, "row", 1)
    own, arrived = lax.optimization_barrier((dot_parts(dense_own, gathered_x), arrived))
    first_blocks = (own + arrived.astype(F32)).reshape(chips, node_rows, -1)
    grad_other = swap(grad_own, "row", 1)
    back_part = back_own + dot_parts(dense_other, grad_other, 0)
    first_blocks, back_part = lax.optimization_barrier((first_blocks, back_part))
    first_sent = [first_blocks[0]] + [block.astype(BF16) for block in first_blocks[1:]]
    back_blocks = back_part.reshape(grid_cols, node_rows, -1)
    back_sent = [back_blocks[k ^ far] for k in range(grid_cols)]
    back_sent = [back_sent[0]] + [block.astype(BF16) for block in back_sent[1:]]
    first_parts = exchange(first_sent, "row", 2, chips - 1)
    back_arrived = in_order(exchange(back_sent, "col", 1, grid_cols // 2), grid_cols // 2)
    back_arrived.pop(grid_cols // 2)
    mean, act, slope, projected = activate(
        first_blocks, in_order(first_parts, chips - 1), chips - 1, first_weight, second_weight
    )
    parts_h = exchange([projected] * grid_cols, "col", 1, grid_cols // 2)

    scale = 1.0 / math.sqrt(node_rows * grid_rows * grid_cols)
    mine, theirs = local_grads(
        mean, act, slope, back_part, back_arrived, second_weight, scale
    )
    mine = (mine + swap(theirs, "row", 1).astype(F32)).astype(BF16)
    _, *parts_h = lax.optimization_barrier((mine, *parts_h))
    parts_h = in_order(lax.optimization_barrier(in_order(parts_h, grid_cols // 2)), grid_cols // 2)
    gathered_h = jnp.concatenate(in_order(parts_h, far), axis=0)
    partner = dot_parts(dense_other, gathered_h).astype(BF16)
    arrived = swap(partner, "row", 1)
    own, arrived = lax.optimization_barrier((dot_parts(dense_own, gathered_h), arrived))
    blocks = (own + arrived.astype(F32)).reshape(chips, node_rows, -1)
    mine = tree_in_order(exchange([mine] * chips, "row", 2, chips - 1), chips - 1).astype(BF16)
    sent = [blocks[0]] + [block.astype(BF16) for block in blocks[1:]]
    output = tree_in_order(exchange(sent, "row", 2, chips - 1), chips - 1).astype(BF16)
    mine = tree_in_order(exchange([mine] * grid_cols, "col", 1, 0), 0)
    first_grad, second_grad = join(mine, swap(mine, "row", 1), first_weight.shape[1])
    return (output, first_grad, second_grad)


def solution(mesh):
    return jax.shard_map(
        on_device,
        mesh=mesh,
        in_specs=(
            P(("row", "col"), None),
            P("row", "col", None, None, None),
            P("row", "col", None, None),
            P("row", "col"),
            P(),
            P(),
            P(("row", "col"), None),
        ),
        out_specs=(P(("row", "col"), None), P(), P()),
        check_vma=False,
    )
```
